32 devices in a mesh: gy: 4 (over y, x), gx: 8 (over z, core).
Axes of the slice: x: 2, y: 2, z: 4, core: 2. Of those that a mesh axis runs over, the one named last changes fastest.
Arguments:
- ocean_state: bfloat16 [1536, 16, 2048], P('gy', None, 'gx'), may hold values from -6 to 6
- atm_blocks: bfloat16 [6144, 16, 128], P(('gy', 'gx')), may hold values from -6 to 6
- dest_tile: int32 [6144, 1], P(('gy', 'gx')), may hold values from 0 to 31; in each aligned block of 192 rows (0 to 191, 192 to 383, ...) at most 12 rows name the same one
- dest_row: int32 [6144], P(('gy', 'gx')), may hold values from 0 to 191
- live_entry: int32 [6144], P(('gy', 'gx')), may hold values 0 or 1
- land_mask: int32 [1536, 2048], P('gy', 'gx'), may hold values 0 or 1
- fold_pair: int32 [8], replicated, may hold values from 0 to 7, as said below
- first_weight: bfloat16 [3, 3, 64, 32], replicated, may hold values from -0.375 to 0.375
- first_bias: float32 [64], replicated, may hold values from -3 to 3
- second_weight: bfloat16 [3, 3, 8, 64], replicated, may hold values from -0.25 to 0.25
- second_bias: float32 [8], replicated, may hold values from -3 to 3
Outputs:
- eddy_forcing: bfloat16 [1536, 8, 2048], P('gy', None, 'gx')
The draws below stay inside these ranges and needn't reach their ends.
Inputs may be any that keep to these rules, and one draw needn't show every extreme that they name: `dest_tile`: at most 12 of the 192 entries held by one device name the same tile, and some device names some tile exactly 12 times. fold_pair[fold_pair[t]] = t and fold_pair[t] != t for every tile t.
All inputs are finite; a program needn't handle non-finite values. No bound on the sum of `live_entry` or of `land_mask` on one device may be relied on, other than what follows from the above.
Results may differ from the reference program's by a relative error of at most 0.005.
Values may be sent and summed in bfloat16 or wider, within the bound.
A program may use at most 192 MiB of HBM per device.

```python
import math
import jax
import jax.numpy as jnp
import numpy as np
from jax import lax

LEV = 4
F = 16
HID = 64
BLOCK = 128
CX = 256
CYH = 192
CAP = 12
BLOCKS = 6144
NLAT = 1536
NLON = 2048
LON_TILES = 8
CIN = 32
OUT = 8
N_GY = 4
N_GX = 8
DEVICES = 32


def draw_fold_pair(key, part):
    order = jax.random.permutation(key, LON_TILES).astype(jnp.int32)
    first_half = order[0::2]
    second_half = order[1::2]
    paired = jnp.zeros((LON_TILES,), jnp.int32)
    paired = paired.at[first_half].set(second_half).at[second_half].set(first_half)
    return paired.astype(jnp.int32)


def place_ends(drawn, own_key, smallest, high):
    longest = drawn.shape.index(max(drawn.shape))
    spots = []
    for shift in (0, 1):
        where = [jax.random.randint(jax.random.fold_in(own_key, axis), (), 0, length) for axis, length in enumerate(drawn.shape)]
        where[longest] = (where[longest] + shift) % drawn.shape[longest]
        spots.append(tuple(where))
    return drawn.at[spots[0]].set(smallest).at[spots[1]].set(high)


def block_scale(key, dims, shards, least, largest):
    gain, own = 1.0, jax.random.fold_in(key, 6)
    for axis_at, blocks in shards:
        heights = jnp.exp(jax.random.uniform(jax.random.fold_in(own, axis_at), (blocks,), jnp.float32, least / len(shards), largest / len(shards)))
        gain = gain * jnp.repeat(heights, dims[axis_at] // blocks).reshape([-1 if axis == axis_at else 1 for axis in range(len(dims))])
    return gain


def routed_block(key, own, number, rows, count, top, limit, slope):
    ranking = jax.random.permutation(key, count)
    packed, common = shares(count, rows * top, limit, slope, True), shares(count, rows * top, limit, slope, False)
    places = jnp.arange(count)

    def named(sizes, turn):
        used = int((sizes > 0).sum())
        fixed = max(1, used // 4)
        moved = fixed + (places - fixed + turn * (used - fixed)) % max(1, count - fixed)
        return jnp.zeros((count,), jnp.int32).at[ranking[jnp.where(places < fixed, places, moved)]].set(jnp.asarray(sizes, jnp.int32))

    sizes = jnp.where(number % 4 == 0, named(packed, number // 4), named(common, number - number // 4 - 1))
    mixed = jax.random.permutation(jax.random.fold_in(own, 3), count)
    donor, taker = mixed[0:count // 2 * 2:2], mixed[1:count // 2 * 2:2]
    slack = jnp.minimum(sizes[donor] - 1, limit - sizes[taker]) // 2
    slack = jnp.where((donor == ranking[0]) | (taker == ranking[0]) | (sizes[taker] == 0), 0, jnp.maximum(slack, 0))
    moved = jax.random.randint(jax.random.fold_in(own, 4), (count // 2,), 0, 1 << 20) % (slack + 1)
    sizes = sizes.at[donor].add(-moved).at[taker].add(moved)
    members = jnp.searchsorted(jnp.cumsum(sizes), jnp.arange(rows * top), side="right").astype(jnp.int32)
    table = members.reshape(top, rows).T
    table = table[jax.random.permutation(jax.random.fold_in(own, 1), rows)]
    turn = jax.random.randint(jax.random.fold_in(own, 2), (rows, 1), 0, top)
    return jnp.take_along_axis(table, (jnp.arange(top)[None, :] + turn) % top, axis=1)


def shares(count, total, most, slope, full):
    portions = [(1 << 20) // math.isqrt(standing ** slope) + 1 for standing in range(1, count + 1)]
    largest = most if full else min(most, max(-(-total // count), total * portions[0] // sum(portions)))
    least = 1 if total - largest >= count - 1 else 0
    holding, rest = [largest] + [least] * (count - 1), total - largest - least * (count - 1)
    while rest > 0:
        movable = [i for i in range(1, count) if holding[i] < largest] or [i for i in range(1, count) if holding[i] < most]
        pool, budget = sum([portions[i] for i in movable]), rest
        for i in movable:
            extra = min(most - holding[i], max(1, budget * portions[i] // pool), rest)
            holding[i] = holding[i] + extra
            rest = rest - extra
    return np.array(holding)


def centred(rng, extent, scale, most, shards=(), kind=jnp.bfloat16):
    entries = jax.random.normal(rng, extent, jnp.float32) * scale
    if len(shards) > 0:
        entries = block_scale(rng, extent, shards, -0.22, 0.18) * entries
    return jnp.clip(entries, min=-most, max=most).astype(kind)


def setup_inputs(seed: int = 0) -> dict:
    arg_keys = jax.random.split(jax.random.key(seed), 12)
    ocean_state = centred(arg_keys[0], (NLAT, 4 * LEV, NLON), 1.0, 6.0, ((0, 4), (2, 8)))
    atm_blocks = centred(arg_keys[1], (BLOCKS, F, BLOCK), 1.0, 6.0, ((0, 32),))
    dest_tile_keys = jax.random.split(jax.random.fold_in(arg_keys[2], 1), BLOCKS // CYH)
    dest_tile_turns = jax.random.permutation(jax.random.fold_in(arg_keys[2], 3), BLOCKS // CYH)
    dest_tile = jax.vmap(lambda own, number: routed_block(jax.random.fold_in(arg_keys[2], 2), own, number, CYH, DEVICES, 1, CAP, 2))(dest_tile_keys, dest_tile_turns).reshape((BLOCKS, 1))
    dest_row = place_ends(jax.random.randint(arg_keys[3], (BLOCKS,), 0, CYH), jax.random.fold_in(arg_keys[3], 1), 0, CYH - 1).astype(jnp.int32)
    live_entry = place_ends((jax.random.randint(arg_keys[4], (BLOCKS,), 0, 8) < 7).astype(jnp.int32), jax.random.fold_in(arg_keys[4], 1), 0, 1)
    land_mask = place_ends((jax.random.randint(arg_keys[5], (NLAT, NLON), 0, 4) < 3).astype(jnp.int32), jax.random.fold_in(arg_keys[5], 1), 0, 1)
    fold_pair = draw_fold_pair(jax.random.fold_in(arg_keys[11], 71), 0)
    first_weight = centred(arg_keys[7], (3, 3, HID, CIN), (9 * CIN) ** -0.5, 0.375)
    first_bias = centred(arg_keys[8], (HID,), 0.5, 3.0, (), jnp.float32)
    second_weight = centred(arg_keys[9], (3, 3, OUT, HID), (9 * HID) ** -0.5, 0.25)
    second_bias = centred(arg_keys[10], (OUT,), 0.5, 3.0, (), jnp.float32)
    return dict(ocean_state=ocean_state, atm_blocks=atm_blocks, dest_tile=dest_tile, dest_row=dest_row, live_entry=live_entry, land_mask=land_mask, fold_pair=fold_pair, first_weight=first_weight, first_bias=first_bias, second_weight=second_weight, second_bias=second_bias)


row_step = 64


def fold_columns(fold_pair):
    columns = (jnp.arange(-1, NLON + 1) % NLON).astype(jnp.int32)
    tiles = (columns // CX).astype(jnp.int32)
    return (jnp.take(fold_pair, tiles) * CX + CX - 1 - columns % CX).astype(jnp.int32)


def convolve(padded, weight):
    count = padded.shape[0] - 2
    total = jnp.zeros((count, weight.shape[2], NLON), jnp.float32)
    for shift_y in range(3):
        for shift_x in range(3):
            total = total + jnp.einsum("oc,ycx->yox", weight[shift_y, shift_x].astype(jnp.float32), padded[shift_y:shift_y + count, :, shift_x:shift_x + NLON].astype(jnp.float32))
    return total


def reference(ocean_state, atm_blocks, dest_tile, dest_row, live_entry, land_mask, fold_pair, first_weight, first_bias, second_weight, second_bias):
    flat_blocks = atm_blocks.reshape(BLOCKS, F * BLOCK).astype(jnp.float32)
    segment = jnp.where(live_entry == 1, dest_tile[:, 0] * CYH + dest_row, N_GY * N_GX * CYH).astype(jnp.int32)
    summed = jax.ops.segment_sum(flat_blocks, segment, num_segments=N_GY * N_GX * CYH + 1)[:-1]
    coarse = summed.astype(jnp.bfloat16).reshape(N_GY, N_GX, CYH, F, BLOCK)
    coarse = coarse.transpose(0, 2, 3, 1, 4).reshape(N_GY * CYH, F, N_GX * BLOCK)
    channel = jnp.arange(CIN)
    in_signs = jnp.where((channel < 2 * LEV) | (channel == 4 * LEV) | (channel == 4 * LEV + 1), -1.0, 1.0).astype(jnp.bfloat16)
    hidden_signs = jnp.ones((HID,), jnp.bfloat16)
    partner = fold_columns(fold_pair)
    mask_values = land_mask.astype(jnp.bfloat16)

    def input_rows(start, count):
        index = (start + jnp.arange(count)).astype(jnp.int32)
        clipped = jnp.clip(index, 0, NLAT - 1).astype(jnp.int32)
        states = jnp.take(ocean_state, clipped, axis=0)
        forcing = jnp.repeat(jnp.take(coarse, (clipped // 2).astype(jnp.int32), axis=0), 2, axis=2)
        mixed = jnp.concatenate([states, forcing], axis=1) * jnp.take(mask_values, clipped, axis=0)[:, None, :]
        return index, mixed

    def pad_rows(index, field_rows, top_row, signs):
        wrapped = jnp.concatenate([field_rows[:, :, -1:], field_rows, field_rows[:, :, :1]], axis=2)
        folded = jnp.take(top_row, partner, axis=1) * signs[:, None]
        inside = ((index >= 0) & (index < NLAT))[:, None, None]
        above = (index == NLAT)[:, None, None]
        return jnp.where(inside, wrapped, jnp.where(above, folded[None], jnp.zeros_like(wrapped)))

    top_index, top_rows = input_rows(NLAT - 1, 1)
    top_input = top_rows[0]
    near_index, near_rows = input_rows(NLAT - 2, 3)
    near_hidden = convolve(pad_rows(near_index, near_rows, top_input, in_signs), first_weight)
    hidden_top = jnp.maximum(near_hidden + first_bias[None, :, None], 0.0).astype(jnp.bfloat16)[0]

    def one_block(number):
        start = (number * row_step).astype(jnp.int32)
        index, field_rows = input_rows(start - 2, row_step + 4)
        hidden = convolve(pad_rows(index, field_rows, top_input, in_signs), first_weight)
        hidden = jnp.maximum(hidden + first_bias[None, :, None], 0.0).astype(jnp.bfloat16)
        hidden_index = (start - 1 + jnp.arange(row_step + 2)).astype(jnp.int32)
        padded_hidden = pad_rows(hidden_index, hidden, hidden_top, hidden_signs)
        result = convolve(padded_hidden, second_weight) + second_bias[None, :, None]
        mask_rows = lax.dynamic_slice_in_dim(mask_values, start, row_step, 0)
        return (result * mask_rows[:, None, :]).astype(jnp.bfloat16)

    blocks = lax.map(one_block, jnp.arange(NLAT // row_step, dtype=jnp.int32))
    return blocks.reshape(NLAT, OUT, NLON)
```

```python
import functools

import jax
import jax.numpy as jnp
import numpy as np
from jax import lax
from jax.experimental import pallas as pl
from jax.experimental.pallas import tpu as pltpu
from jax.sharding import PartitionSpec as P

MESH = pl.DeviceIdType.MESH
R1 = 6
R2 = 6
f32 = jnp.float32
bf16 = jnp.bfloat16


def vmem():
    return pl.BlockSpec(memory_space=pltpu.VMEM)


def smem():
    return pl.BlockSpec(memory_space=pltpu.SMEM)


def anym():
    return pl.BlockSpec(memory_space=pl.ANY)


def pack_kernel(cap, tile_ref, row_ref, live_ref, atm_ref, out_ref, rows_ref, count):
    devices = count.shape[0]

    def clear(i, _):
        count[i] = 0
        return 0

    def clear_rows(i, _):
        rows_ref[i] = -1
        return 0

    lax.fori_loop(0, devices, clear, 0)
    lax.fori_loop(0, rows_ref.shape[0], clear_rows, 0, unroll=8)

    def place(e, _):
        @pl.when(live_ref[e] == 1)
        def _():
            t = tile_ref[e]
            c = count[t]
            count[t] = c + 1
            slot = t * cap + c
            rows_ref[slot] = row_ref[e]
            out_ref[slot] = atm_ref[e]

        return 0

    lax.fori_loop(0, atm_ref.shape[0], place, 0)


def combine_kernel(rows_ref, blocks_ref, state_ref, mask_ref, up_ref, inp_ref, cols_ref, acc, up):
    half = acc.shape[0]
    tile_rows, levels = state_ref.shape[0], state_ref.shape[1]
    acc[...] = jnp.zeros_like(acc)

    def add(s, _):
        r = rows_ref[s]

        @pl.when(r >= 0)
        def _():
            acc[r] += blocks_ref[s].astype(f32)

        return 0

    lax.fori_loop(0, rows_ref.shape[0], add, 0, unroll=4)

    def spread(i, _):
        piece = acc[pl.ds(i * 8, 8)].astype(bf16).reshape(8 * 16, 128)
        wide = jnp.dot(piece, up_ref[...], preferred_element_type=f32)
        up[pl.ds(i * 8, 8)] = wide.reshape(8, 16, 256)
        return 0

    lax.fori_loop(0, half // 8, spread, 0)

    lane = lax.broadcasted_iota(jnp.int32, (32, 128), 1)

    def rows8(i, carry):
        lo, hi = carry
        m = mask_ref[pl.ds(i * 8, 8), :].astype(f32)
        for k in range(8):
            y = i * 8 + k
            mk = jnp.broadcast_to(m[k : k + 1, :], (16, 256))
            a = state_ref[y].astype(f32) * mk
            b = up[i * 4 + k // 2] * mk
            full = jnp.concatenate([a, b], axis=0)
            inp_ref[y] = full.astype(bf16)
            at = lax.rem(2 * y, 128)
            here = (lane >> 1) == lax.rem(y, 64)
            lo = jnp.where(here, pltpu.roll(full[:, :128], at, 1), lo)
            hi = jnp.where(here, pltpu.roll(full[:, 128:], lax.rem(at + 2, 128), 1), hi)
        return lo, hi

    zero = jnp.zeros((32, 128), f32)

    def tile(t, _):
        lo, hi = lax.fori_loop(t * 8, t * 8 + 8, rows8, (zero, zero))
        cols_ref[0, t] = lo.astype(bf16)
        cols_ref[1, t] = hi.astype(bf16)
        return 0

    lax.fori_loop(0, tile_rows // 64, tile, 0)


def exchange_kernel(g_y, g_x, cols_ref, inp_ref, from_cols, rows_s, rows_n, top_all, send, recv, own):
    gy, gx = lax.axis_index("gy"), lax.axis_index("gx")
    n_rows = inp_ref.shape[0]
    west, east = lax.rem(gx + g_x - 1, g_x), lax.rem(gx + 1, g_x)
    low, high = inp_ref.at[pl.ds(0, 2)], inp_ref.at[pl.ds(n_rows - 2, 2)]
    is_top = gy == g_y - 1
    barrier = pltpu.get_barrier_semaphore()

    def copy(src, dst, s, r, y, x):
        return pltpu.make_async_remote_copy(
            src_ref=src, dst_ref=dst, send_sem=send.at[s], recv_sem=recv.at[r], device_id=(y, x), device_id_type=MESH
        )

    def signal(y, x):
        pl.semaphore_signal(barrier, inc=1, device_id=(y, x), device_id_type=MESH)

    sides = (west, gx, east)

    @pl.when(gy > 0)
    def _():
        for x in sides:
            signal(gy - 1, x)

    @pl.when(gy < g_y - 1)
    def _():
        for x in sides:
            signal(gy + 1, x)
        for x in (west, east):
            signal(gy, x)

    @pl.when(is_top)
    def _():
        def one(d, _):
            signal(gy, lax.rem(gx + d, g_x))
            return 0

        lax.fori_loop(1, g_x, one, 0)

    top, bottom = is_top.astype(jnp.int32), (gy == 0).astype(jnp.int32)
    pl.semaphore_wait(barrier, top * (g_x - 1) + (1 - top) * 5 + (1 - bottom) * 3)

    to_west = copy(cols_ref.at[0], from_cols.at[1], 0, 1, gy, west)
    to_east = copy(cols_ref.at[1], from_cols.at[0], 1, 0, gy, east)
    to_south = [copy(low, rows_n.at[2 - k], 2 + k, 5 + 2 - k, gy - 1, sides[k]) for k in range(3)]
    to_north = [copy(high, rows_s.at[2 - k], 5 + k, 2 + 2 - k, gy + 1, sides[k]) for k in range(3)]
    mine = pltpu.make_async_copy(high, top_all.at[gx], own)

    def top_copy(d):
        return copy(high, top_all.at[gx], 8 + d, 8 + d, gy, lax.rem(gx + d, g_x))

    @pl.when(is_top)
    def _():
        def one(d, _):
            top_copy(d).start()
            return 0

        mine.start()
        lax.fori_loop(1, g_x, one, 0)

    @pl.when(gy > 0)
    def _():
        for c in to_south:
            c.start()

    @pl.when(gy < g_y - 1)
    def _():
        for c in to_north:
            c.start()

    to_west.start()
    to_east.start()
    to_west.wait()
    to_east.wait()

    @pl.when(gy > 0)
    def _():
        for c in to_south:
            c.wait_send()
        for k in range(3):
            copy(high, rows_s.at[k], 5, 2 + k, gy, west).wait_recv()

    @pl.when(gy < g_y - 1)
    def _():
        for c in to_north:
            c.wait_send()
        for k in range(3):
            copy(low, rows_n.at[k], 2, 5 + k, gy, west).wait_recv()

    @pl.when(is_top)
    def _():
        def one(d, _):
            c = top_copy(d)
            c.wait_send()
            src = lax.rem(gx + g_x - d, g_x)
            copy(high, top_all.at[src], 8 + d, 8 + d, gy, src).wait_recv()
            return 0

        lax.fori_loop(1, g_x, one, 0)
        mine.wait()


def roll(x, shift, axis=1):
    if isinstance(shift, int):
        shift = shift % x.shape[axis]
        if shift == 0:
            return x
    return pltpu.roll(x, shift, axis)


def conv_kernel(
    g_y, g_x, fold_ref, inp_ref, cols_ref, from_ref, rs_ref, rn_ref, top_ref, mask_ref, w1_ref, w1s_ref, b1_ref, w2_ref,
    w2e_ref, b2_ref, sign_ref, out_ref, x_ref, xl_ref, xr_ref, h_ref, north, south, edge, pedge, sem,
):
    gy, gx = lax.axis_index("gy"), lax.axis_index("gx")
    rows = out_ref.shape[0]
    hid = w1s_ref.shape[0]
    is_top = gy == g_y - 1
    load = pltpu.make_async_copy(inp_ref, x_ref.at[pl.ds(2, rows)], sem)
    load.start()
    lane256 = lax.broadcasted_iota(jnp.int32, (32, 256), 1)
    lane128 = lax.broadcasted_iota(jnp.int32, (32, 128), 1)
    back = (
        lax.broadcasted_iota(jnp.int32, (256, 256), 0) + lax.broadcasted_iota(jnp.int32, (256, 256), 1) == 255
    ).astype(bf16)

    def mirror(v):
        return jnp.dot(v, back, preferred_element_type=f32)

    def top_row(t):
        return mirror(top_ref[t, 1]) * sign_ref[...]

    def put(x, west, east):
        left = jnp.where(lane256 == 0, jnp.concatenate([west, west], axis=1), roll(x, 1))
        right = jnp.where(lane256 == 255, jnp.concatenate([east, east], axis=1), roll(x, -1))
        return left, right

    def side_rows(first, mid, last):
        return put(mid, roll(first[:, 128:], 1), roll(last[:, :128], -1))

    for j in range(2):
        for k in range(3):
            south[k, j] = jnp.where(gy > 0, rs_ref[k, j].astype(f32), 0.0)

    @pl.when(jnp.logical_not(is_top))
    def _():
        for j in range(2):
            for k in range(3):
                north[k, j] = rn_ref[k, j].astype(f32)

    @pl.when(is_top)
    def _():
        for k in range(3):
            t = fold_ref[lax.rem(gx + g_x - 1 + k, g_x)]
            north[k, 0] = top_row(t)
            north[k, 1] = jnp.zeros((32, 256), f32)

    def ext_hi(r0, r1, s0, s1):
        return jnp.where(lane128 >= 126, r1, roll(r0, -2)), jnp.where(lane128 < 2, roll(s0, 2), roll(s1, 4))

    def ext_lo(r0, r1, s0, s1):
        return jnp.where(lane128 >= 126, roll(r1, 126), roll(r0, 124)), jnp.where(lane128 < 2, s0, roll(s1, 2))

    def strip(body, ends):
        first, last = ends
        return jnp.concatenate([first] + [body[t].astype(f32) for t in range(rows // 64)] + [last], axis=1)

    hi, lo = slice(128, 256), slice(0, 128)
    far_w = strip(from_ref.at[0], ext_hi(south[0, 0][:, hi], south[0, 1][:, hi], north[0, 0][:, hi], north[0, 1][:, hi]))
    own_w = strip(cols_ref.at[0], ext_lo(south[1, 0][:, lo], south[1, 1][:, lo], north[1, 0][:, lo], north[1, 1][:, lo]))
    own_e = strip(cols_ref.at[1], ext_hi(south[1, 0][:, hi], south[1, 1][:, hi], north[1, 0][:, hi], north[1, 1][:, hi]))
    far_e = strip(from_ref.at[1], ext_lo(south[2, 0][:, lo], south[2, 1][:, lo], north[2, 0][:, lo], north[2, 1][:, lo]))

    def hidden_of(parts):
        stack = jnp.concatenate([p.astype(bf16) for p in parts], axis=0)
        total = jnp.dot(w1s_ref[...], stack, preferred_element_type=f32)
        return jnp.maximum(total + b1_ref[...], 0.0)

    west_parts, east_parts = [], []
    for u in range(3):
        s = -2 * (u - 1)
        west_parts += [roll(far_w, s), roll(far_w, s - 1), roll(own_w, s)]
        east_parts += [roll(own_e, s - 1), roll(far_e, s), roll(far_e, s - 1)]
    edge_lane = lax.broadcasted_iota(jnp.int32, (hid, 128 * (rows // 64 + 2)), 1)
    live = (edge_lane >= 128) | (gy > 0)
    edge[0] = jnp.where(live, hidden_of(west_parts), 0.0)
    edge[1] = jnp.where(live, hidden_of(east_parts), 0.0)

    load.wait()
    for j in range(2):
        for at, src in ((j, south), (rows + 2 + j, north)):
            left, right = side_rows(src[0, j], src[1, j], src[2, j])
            x_ref[at] = src[1, j].astype(bf16)
            xl_ref[at] = left.astype(bf16)
            xr_ref[at] = right.astype(bf16)
    for at in range(rows + 4, x_ref.shape[0]):
        for r in (x_ref, xl_ref, xr_ref):
            r[at] = jnp.zeros((32, 256), bf16)

    def shift_rows(i, _):
        t = i // 8
        wt, et = from_ref[0, t].astype(f32), from_ref[1, t].astype(f32)
        for k in range(8):
            y = i * 8 + k
            at = lax.rem(2 * y, 128)
            west = roll(wt, 127 - at)
            east = roll(et, 127 - at)
            left, right = put(x_ref[y + 2].astype(f32), west, east)
            xl_ref[y + 2] = left.astype(bf16)
            xr_ref[y + 2] = right.astype(bf16)
        return 0

    lax.fori_loop(0, rows // 8, shift_rows, 0)

    bias1 = jnp.concatenate([b1_ref[...]] * R1, axis=0)

    def hidden_rows(i, _):
        total = jnp.zeros((R1 * hid, 256), f32)
        for v, r in enumerate((xl_ref, x_ref, xr_ref)):
            piece = r[pl.ds(i * R1, R1 + 2)].reshape((R1 + 2) * 32, 256)
            total = total + jnp.dot(w1_ref[v], piece, preferred_element_type=f32)
        total = jnp.maximum(total + bias1, 0.0)
        h_ref[pl.ds(i * R1, R1)] = total.astype(bf16).reshape(R1, hid, 256)
        return 0

    lax.fori_loop(0, h_ref.shape[0] // R1, hidden_rows, 0)

    @pl.when(gy == 0)
    def _():
        h_ref[0] = jnp.zeros((hid, 256), bf16)

    @pl.when(is_top)
    def _():
        for k in range(3):
            q = fold_ref[lax.rem(gx + g_x - 1 + k, g_x)]
            qw, qe = lax.rem(q + g_x - 1, g_x), lax.rem(q + 1, g_x)
            parts = []
            for j in range(2):
                a, b, c = (top_ref[t, j].astype(f32) for t in (qw, q, qe))
                left, right = side_rows(a, b, c)
                parts += [left, b, right]
            a, b, c = (top_row(fold_ref[t]) for t in (qw, q, qe))
            left, right = side_rows(a, b, c)
            parts += [left, b, right]
            folded = mirror(hidden_of(parts).astype(bf16))
            if k == 1:
                h_ref[rows + 1] = folded.astype(bf16)
            else:
                tiles = rows // 64 + 1
                e = 0 if k == 0 else 1
                piece = roll(folded[:, 128:], 1) if k == 0 else folded[:, :128]
                edge[e, :, 128 * tiles :] = piece

    for e in range(2):
        h = edge[e]
        stack = jnp.concatenate([roll(h, -2 * (u - 1)).astype(bf16) for u in range(3)], axis=0)
        sums = jnp.dot(w2e_ref[e], stack, preferred_element_type=f32)
        for t in range(rows // 64 + 2):
            pedge[e, t] = sums[:, 128 * t : 128 * t + 128]

    outs = out_ref.shape[1]
    lane8 = lax.broadcasted_iota(jnp.int32, (outs, 256), 1)
    bias2 = b2_ref[...]

    def out_rows(i, _):
        piece = h_ref[pl.ds(i * R2, R2 + 2)].reshape((R2 + 2) * hid, 256)
        sums = jnp.dot(w2_ref[...], piece, preferred_element_type=f32)
        for k in range(R2):
            y = i * R2 + k
            t = y // 64 + 1
            at = lax.rem(2 * y, 128)
            a, b, c = (sums[(v * R2 + k) * outs : (v * R2 + k + 1) * outs] for v in range(3))
            west = roll(pedge[0, t], lax.rem(128 - at, 128))
            east = roll(pedge[1, t], 127 - at)
            a = jnp.where(lane8 == 0, jnp.concatenate([west, west], axis=1), roll(a, 1))
            c = jnp.where(lane8 == 255, jnp.concatenate([east, east], axis=1), roll(c, -1))
            m = jnp.broadcast_to(mask_ref[pl.ds(y, 1), :].astype(f32), (outs, 256))
            out_ref[y] = ((a + b + c + bias2) * m).astype(bf16)
        return 0

    lax.fori_loop(0, rows // R2, out_rows, 0)


def per_device(
    ocean_state, atm_blocks, dest_tile, dest_row, live_entry, land_mask, fold_pair, first_weight, first_bias,
    second_weight, second_bias,
):
    rows, levels4, cols = ocean_state.shape
    held, fields, block_cols = atm_blocks.shape
    g_y, g_x = lax.axis_size("gy"), lax.axis_size("gx")
    devices = g_y * g_x
    cap = max(2, 2 * held // devices)
    slots = devices * cap
    half = rows // 2
    cin = levels4 + fields
    hid, outs = first_weight.shape[2], second_weight.shape[2]
    tiles = rows // 64
    params = functools.partial(pltpu.CompilerParams, vmem_limit_bytes=60 * 2**20)

    outgoing, outgoing_rows = pl.pallas_call(
        functools.partial(pack_kernel, cap),
        out_shape=(jax.ShapeDtypeStruct((slots, fields, block_cols), bf16), jax.ShapeDtypeStruct((slots,), jnp.int32)),
        in_specs=[smem(), smem(), smem(), vmem()],
        out_specs=(vmem(), smem()),
        scratch_shapes=[pltpu.SMEM((devices,), jnp.int32)],
        name="pack",
    )(dest_tile.reshape(held), dest_row, live_entry, atm_blocks)
    incoming, incoming_rows = (
        lax.all_to_all(a, ("gy", "gx"), split_axis=0, concat_axis=0, tiled=True)
        for a in (outgoing.reshape(devices, cap, fields, block_cols), outgoing_rows.reshape(devices, cap))
    )
    spread = np.zeros((block_cols, cols), np.float32)
    spread[np.arange(cols) // 2, np.arange(cols)] = 1
    inputs, edge_cols = pl.pallas_call(
        combine_kernel,
        out_shape=(
            jax.ShapeDtypeStruct((rows, cin, cols), bf16),
            jax.ShapeDtypeStruct((2, tiles, cin, 128), bf16),
        ),
        in_specs=[smem()] + [vmem()] * 4,
        out_specs=(vmem(), vmem()),
        scratch_shapes=[pltpu.VMEM((half, fields, block_cols), f32), pltpu.VMEM((half, fields, cols), f32)],
        compiler_params=params(),
        name="combine",
    )(
        incoming_rows.reshape(slots), incoming.reshape(slots, fields, block_cols), ocean_state, land_mask,
        jnp.asarray(spread, bf16),
    )

    from_cols, rows_s, rows_n, top_all = pl.pallas_call(
        functools.partial(exchange_kernel, g_y, g_x),
        out_shape=(
            jax.ShapeDtypeStruct((2, tiles, cin, 128), bf16),
            jax.ShapeDtypeStruct((3, 2, cin, cols), bf16),
            jax.ShapeDtypeStruct((3, 2, cin, cols), bf16),
            jax.ShapeDtypeStruct((g_x, 2, cin, cols), bf16),
        ),
        in_specs=[anym(), anym()],
        out_specs=(anym(),) * 4,
        scratch_shapes=[
            pltpu.SemaphoreType.DMA((8 + g_x,)), pltpu.SemaphoreType.DMA((8 + g_x,)), pltpu.SemaphoreType.DMA,
        ],
        compiler_params=pltpu.CompilerParams(collective_id=0, has_side_effects=True),
        name="exchange",
    )(edge_cols, inputs)

    def band(r):
        t = np.zeros((3, r, r + 2), np.float32)
        for u in range(3):
            t[u, np.arange(r), np.arange(r) + u] = 1
        return jnp.asarray(t, bf16)

    w1 = jnp.einsum("urs,uvoc->vrosc", band(R1), first_weight).reshape(3, R1 * hid, (R1 + 2) * cin)
    w1s = first_weight.transpose(2, 0, 1, 3).reshape(hid, 9 * cin)
    w2 = jnp.einsum("urs,uvoc->vrosc", band(R2), second_weight).reshape(3 * R2 * outs, (R2 + 2) * hid)
    w2e = jnp.stack([second_weight[:, v].transpose(1, 0, 2).reshape(outs, 3 * hid) for v in (0, 2)])
    levels = levels4 // 4
    channel = np.arange(cin)
    negative = (channel < 2 * levels) | (channel == levels4) | (channel == levels4 + 1)
    signs = jnp.asarray(np.where(negative, -1.0, 1.0).astype(np.float32)[:, None])
    h_rows = -(-(rows + 2) // R1) * R1
    x_shape = (h_rows + 2, cin, cols)
    return pl.pallas_call(
        functools.partial(conv_kernel, g_y, g_x),
        out_shape=jax.ShapeDtypeStruct((rows, outs, cols), bf16),
        in_specs=[smem(), anym()] + [vmem()] * 13,
        out_specs=vmem(),
        scratch_shapes=[
            pltpu.VMEM(x_shape, bf16),
            pltpu.VMEM(x_shape, bf16),
            pltpu.VMEM(x_shape, bf16),
            pltpu.VMEM((h_rows, hid, cols), bf16),
            pltpu.VMEM((3, 2, cin, cols), f32),
            pltpu.VMEM((3, 2, cin, cols), f32),
            pltpu.VMEM((2, hid, 128 * (tiles + 2)), f32),
            pltpu.VMEM((2, tiles + 2, outs, 128), f32),
            pltpu.SemaphoreType.DMA,
        ],
        compiler_params=params(),
        name="conv",
    )(
        fold_pair, inputs, edge_cols, from_cols, rows_s, rows_n, top_all, land_mask, w1, w1s, first_bias[:, None], w2,
        w2e, second_bias[:, None], signs,
    )


def solution(mesh):
    return jax.shard_map(
        per_device,
        mesh=mesh,
        in_specs=(
            P("gy", None, "gx"),
            P(("gy", "gx"), None, None),
            P(("gy", "gx"), None),
            P(("gy", "gx")),
            P(("gy", "gx")),
            P("gy", "gx"),
            P(),
            P(),
            P(),
            P(),
            P(),
        ),
        out_specs=P("gy", None, "gx"),
        check_vma=False,
    )
```

```python
import functools

import jax
import jax.numpy as jnp
import numpy as np
from jax import lax
from jax.experimental import pallas as pl
from jax.experimental.pallas import tpu as pltpu
from jax.sharding import PartitionSpec as P

MESH = pl.DeviceIdType.MESH
R1 = 6
R2 = 6
GROUP = 5
f32 = jnp.float32
bf16 = jnp.bfloat16


def vmem():
    return pl.BlockSpec(memory_space=pltpu.VMEM)


def smem():
    return pl.BlockSpec(memory_space=pltpu.SMEM)


def anym():
    return pl.BlockSpec(memory_space=pl.ANY)


def pack_kernel(tile_ref, row_ref, live_ref, atm_ref, out_ref, count, names, *, empty):
    devices, cap = out_ref.shape[0], out_ref.shape[1] - 1
    names[...] = jnp.full(names.shape, empty, f32)
    lane = lax.broadcasted_iota(jnp.int32, (8, 128), 1)

    def clear(i, _):
        count[i] = 0
        return 0

    lax.fori_loop(0, devices, clear, 0, unroll=8)

    def place(e, _):
        t, live = tile_ref[e], live_ref[e]
        c = count[t]
        count[t] = c + live
        out_ref[t, jnp.where(live == 1, c, cap)] = atm_ref[e]
        names[t] = jnp.where(lane == jnp.where(live == 1, c, -1), row_ref[e].astype(f32), names[t])
        return 0

    lax.fori_loop(0, atm_ref.shape[0], place, 0, unroll=8)

    def name(t, _):
        out_ref[t, cap] = jnp.concatenate([names[t], names[t]], axis=0).astype(bf16)
        return 0

    lax.fori_loop(0, devices, name, 0, unroll=4)


def combine_kernel(rows_ref, blocks_ref, state_ref, mask_ref, up_ref, inp_ref, cols_ref, acc, up):
    half = acc.shape[0] - 1
    slots = blocks_ref.shape[1] - 1
    tile_rows, levels = state_ref.shape[0], state_ref.shape[1]
    acc[...] = jnp.zeros_like(acc)

    def add(d, _):
        for k in range(slots):
            r = rows_ref[d * slots + k]
            acc[r] += blocks_ref[d, k].astype(f32)
        return 0

    lax.fori_loop(0, blocks_ref.shape[0], add, 0)

    def spread(i, _):
        piece = acc[pl.ds(i * 8, 8)].astype(bf16).reshape(8 * 16, 128)
        wide = jnp.dot(piece, up_ref[...], preferred_element_type=f32)
        up[pl.ds(i * 8, 8)] = wide.reshape(8, 16, 256)
        return 0

    lax.fori_loop(0, half // 8, spread, 0)

    lane = lax.broadcasted_iota(jnp.int32, (32, 128), 1)

    def rows8(i, carry):
        lo, hi = carry
        m = mask_ref[pl.ds(i * 8, 8), :].astype(f32)
        for k in range(8):
            y = i * 8 + k
            mk = jnp.broadcast_to(m[k : k + 1, :], (16, 256))
            a = state_ref[y].astype(f32) * mk
            b = up[i * 4 + k // 2] * mk
            full = jnp.concatenate([a, b], axis=0)
            inp_ref[y] = full.astype(bf16)
            at = lax.rem(2 * y, 128)
            here = (lane >> 1) == lax.rem(y, 64)
            lo = jnp.where(here, pltpu.roll(full[:, :128], at, 1), lo)
            hi = jnp.where(here, pltpu.roll(full[:, 128:], lax.rem(at + 2, 128), 1), hi)
        return lo, hi

    zero = jnp.zeros((32, 128), f32)

    def tile(t, _):
        lo, hi = lax.fori_loop(t * 8, t * 8 + 8, rows8, (zero, zero))
        cols_ref[0, t] = lo.astype(bf16)
        cols_ref[1, t] = hi.astype(bf16)
        return 0

    lax.fori_loop(0, tile_rows // 64, tile, 0)


def exchange_kernel(g_y, g_x, cols_ref, inp_ref, from_cols, rows_s, rows_n, top_all, send, recv, own):
    gy, gx = lax.axis_index("gy"), lax.axis_index("gx")
    n_rows = inp_ref.shape[0]
    west, east = lax.rem(gx + g_x - 1, g_x), lax.rem(gx + 1, g_x)
    low, high = inp_ref.at[pl.ds(0, 2)], inp_ref.at[pl.ds(n_rows - 2, 2)]
    is_top = gy == g_y - 1
    barrier = pltpu.get_barrier_semaphore()

    def copy(src, dst, s, r, y, x):
        return pltpu.make_async_remote_copy(
            src_ref=src, dst_ref=dst, send_sem=send.at[s], recv_sem=recv.at[r], device_id=(y, x), device_id_type=MESH
        )

    def signal(y, x):
        pl.semaphore_signal(barrier, inc=1, device_id=(y, x), device_id_type=MESH)

    sides = (west, gx, east)

    @pl.when(gy > 0)
    def _():
        for x in sides:
            signal(gy - 1, x)

    @pl.when(gy < g_y - 1)
    def _():
        for x in sides:
            signal(gy + 1, x)
        for x in (west, east):
            signal(gy, x)

    @pl.when(is_top)
    def _():
        def one(d, _):
            signal(gy, lax.rem(gx + d, g_x))
            return 0

        lax.fori_loop(1, g_x, one, 0)

    top, bottom = is_top.astype(jnp.int32), (gy == 0).astype(jnp.int32)
    pl.semaphore_wait(barrier, top * (g_x - 1) + (1 - top) * 5 + (1 - bottom) * 3)

    to_west = copy(cols_ref.at[0], from_cols.at[1], 0, 1, gy, west)
    to_east = copy(cols_ref.at[1], from_cols.at[0], 1, 0, gy, east)
    to_south = [copy(low, rows_n.at[2 - k], 2 + k, 5 + 2 - k, gy - 1, sides[k]) for k in range(3)]
    to_north = [copy(high, rows_s.at[2 - k], 5 + k, 2 + 2 - k, gy + 1, sides[k]) for k in range(3)]
    mine = pltpu.make_async_copy(high, top_all.at[gx], own)

    def top_copy(d):
        return copy(high, top_all.at[gx], 8 + d, 8 + d, gy, lax.rem(gx + d, g_x))

    @pl.when(is_top)
    def _():
        def one(d, _):
            top_copy(d).start()
            return 0

        mine.start()
        lax.fori_loop(1, g_x, one, 0)

    @pl.when(gy > 0)
    def _():
        for c in to_south:
            c.start()

    @pl.when(gy < g_y - 1)
    def _():
        for c in to_north:
            c.start()

    to_west.start()
    to_east.start()
    to_west.wait()
    to_east.wait()

    @pl.when(gy > 0)
    def _():
        for c in to_south:
            c.wait_send()
        for k in range(3):
            copy(high, rows_s.at[k], 5, 2 + k, gy, west).wait_recv()

    @pl.when(gy < g_y - 1)
    def _():
        for c in to_north:
            c.wait_send()
        for k in range(3):
            copy(low, rows_n.at[k], 2, 5 + k, gy, west).wait_recv()

    @pl.when(is_top)
    def _():
        def one(d, _):
            c = top_copy(d)
            c.wait_send()
            src = lax.rem(gx + g_x - d, g_x)
            copy(high, top_all.at[src], 8 + d, 8 + d, gy, src).wait_recv()
            return 0

        lax.fori_loop(1, g_x, one, 0)
        mine.wait()


def roll(x, shift, axis=1):
    if isinstance(shift, int):
        shift = shift % x.shape[axis]
        if shift == 0:
            return x
    return pltpu.roll(x, shift, axis)


def conv_kernel(
    g_y, g_x, fold_ref, inp_ref, cols_ref, from_ref, rs_ref, rn_ref, top_ref, mask_ref, w1_ref, w1s_ref, b1_ref, w2_ref,
    w2e_ref, b2_ref, sign_ref, out_ref, x_ref, far_ref, h_ref, north, south, edge, pedge, sem,
):
    gy, gx = lax.axis_index("gy"), lax.axis_index("gx")
    rows = out_ref.shape[0]
    hid = w1s_ref.shape[0]
    is_top = gy == g_y - 1
    load = pltpu.make_async_copy(inp_ref, x_ref.at[pl.ds(2, rows)], sem)
    load.start()
    lane256 = lax.broadcasted_iota(jnp.int32, (32, 256), 1)
    lane128 = lax.broadcasted_iota(jnp.int32, (32, 128), 1)
    back = (
        lax.broadcasted_iota(jnp.int32, (256, 256), 0) + lax.broadcasted_iota(jnp.int32, (256, 256), 1) == 255
    ).astype(bf16)

    def mirror(v):
        return jnp.dot(v, back, preferred_element_type=f32)

    def top_row(t):
        return mirror(top_ref[t, 1]) * sign_ref[...]

    def put(x, west, east):
        left = jnp.where(lane256 == 0, jnp.concatenate([west, west], axis=1), roll(x, 1))
        right = jnp.where(lane256 == 255, jnp.concatenate([east, east], axis=1), roll(x, -1))
        return left, right

    def side_rows(first, mid, last):
        return put(mid, roll(first[:, 128:], 1), roll(last[:, :128], -1))

    for j in range(2):
        for k in range(3):
            south[k, j] = jnp.where(gy > 0, rs_ref[k, j].astype(f32), 0.0)

    @pl.when(jnp.logical_not(is_top))
    def _():
        for j in range(2):
            for k in range(3):
                north[k, j] = rn_ref[k, j].astype(f32)

    @pl.when(is_top)
    def _():
        for k in range(3):
            t = fold_ref[lax.rem(gx + g_x - 1 + k, g_x)]
            north[k, 0] = top_row(t)
            north[k, 1] = jnp.zeros((32, 256), f32)

    def ext_hi(r0, r1, s0, s1):
        return jnp.where(lane128 >= 126, r1, roll(r0, -2)), jnp.where(lane128 < 2, roll(s0, 2), roll(s1, 4))

    def ext_lo(r0, r1, s0, s1):
        return jnp.where(lane128 >= 126, roll(r1, 126), roll(r0, 124)), jnp.where(lane128 < 2, s0, roll(s1, 2))

    def strip(body, ends):
        first, last = ends
        return jnp.concatenate([first] + [body[t].astype(f32) for t in range(rows // 64)] + [last], axis=1)

    hi, lo = slice(128, 256), slice(0, 128)
    far_w = strip(from_ref.at[0], ext_hi(south[0, 0][:, hi], south[0, 1][:, hi], north[0, 0][:, hi], north[0, 1][:, hi]))
    own_w = strip(cols_ref.at[0], ext_lo(south[1, 0][:, lo], south[1, 1][:, lo], north[1, 0][:, lo], north[1, 1][:, lo]))
    own_e = strip(cols_ref.at[1], ext_hi(south[1, 0][:, hi], south[1, 1][:, hi], north[1, 0][:, hi], north[1, 1][:, hi]))
    far_e = strip(from_ref.at[1], ext_lo(south[2, 0][:, lo], south[2, 1][:, lo], north[2, 0][:, lo], north[2, 1][:, lo]))

    def hidden_of(parts):
        stack = jnp.concatenate([p.astype(bf16) for p in parts], axis=0)
        total = jnp.dot(w1s_ref[...], stack, preferred_element_type=f32)
        return jnp.maximum(total + b1_ref[...], 0.0)

    for t in range(rows // 64 + 2):
        far_ref[0, t] = far_w[:, 128 * t : 128 * t + 128]
        far_ref[1, t] = far_e[:, 128 * t : 128 * t + 128]
    west_parts, east_parts = [], []
    for u in range(3):
        s = -2 * (u - 1)
        west_parts += [roll(far_w, s), roll(far_w, s - 1), roll(own_w, s)]
        east_parts += [roll(own_e, s - 1), roll(far_e, s), roll(far_e, s - 1)]
    edge_lane = lax.broadcasted_iota(jnp.int32, (hid, 128 * (rows // 64 + 2)), 1)
    live = (edge_lane >= 128) | (gy > 0)
    edge[0] = jnp.where(live, hidden_of(west_parts), 0.0)
    edge[1] = jnp.where(live, hidden_of(east_parts), 0.0)

    load.wait()
    for j in range(2):
        x_ref[j] = south[1, j].astype(bf16)
        x_ref[rows + 2 + j] = north[1, j].astype(bf16)
    for at in range(rows + 4, x_ref.shape[0]):
        x_ref[at] = jnp.zeros((32, 256), bf16)

    bias1 = jnp.concatenate([b1_ref[...]] * R1, axis=0)
    weights = jnp.concatenate([w1_ref[v] for v in range(3)], axis=1)

    def hidden_rows(i, _):
        first = i * (GROUP * R1)
        shifted = []
        for k in range(GROUP * R1 + 2):
            at = 124 + 2 * (first + k)
            t, lane = at // 128, lax.rem(at, 128)
            x = x_ref[first + k]
            left, right = put(x.astype(f32), roll(far_ref[0, t], 127 - lane), roll(far_ref[1, t], 127 - lane))
            shifted.append((left.astype(bf16), x, right.astype(bf16)))
        for b in range(GROUP):
            piece = jnp.concatenate([row[v] for v in range(3) for row in shifted[b * R1 : b * R1 + R1 + 2]], axis=0)
            total = jnp.dot(weights, piece, preferred_element_type=f32)
            total = jnp.maximum(total + bias1, 0.0)
            h_ref[pl.ds(first + b * R1, R1)] = total.astype(bf16).reshape(R1, hid, 256)
        return 0

    lax.fori_loop(0, h_ref.shape[0] // (GROUP * R1), hidden_rows, 0)

    @pl.when(gy == 0)
    def _():
        h_ref[0] = jnp.zeros((hid, 256), bf16)

    @pl.when(is_top)
    def _():
        for k in range(3):
            q = fold_ref[lax.rem(gx + g_x - 1 + k, g_x)]
            qw, qe = lax.rem(q + g_x - 1, g_x), lax.rem(q + 1, g_x)
            parts = []
            for j in range(2):
                a, b, c = (top_ref[t, j].astype(f32) for t in (qw, q, qe))
                left, right = side_rows(a, b, c)
                parts += [left, b, right]
            a, b, c = (top_row(fold_ref[t]) for t in (qw, q, qe))
            left, right = side_rows(a, b, c)
            parts += [left, b, right]
            folded = mirror(hidden_of(parts).astype(bf16))
            if k == 1:
                h_ref[rows + 1] = folded.astype(bf16)
            else:
                tiles = rows // 64 + 1
                e = 0 if k == 0 else 1
                piece = roll(folded[:, 128:], 1) if k == 0 else folded[:, :128]
                edge[e, :, 128 * tiles :] = piece

    for e in range(2):
        h = edge[e]
        stack = jnp.concatenate([roll(h, -2 * (u - 1)).astype(bf16) for u in range(3)], axis=0)
        sums = jnp.dot(w2e_ref[e], stack, preferred_element_type=f32)
        for t in range(rows // 64 + 2):
            pedge[e, t] = sums[:, 128 * t : 128 * t + 128]

    outs = out_ref.shape[1]
    lane8 = lax.broadcasted_iota(jnp.int32, (outs, 256), 1)
    bias2 = b2_ref[...]

    def out_rows(i, _):
        piece = h_ref[pl.ds(i * R2, R2 + 2)].reshape((R2 + 2) * hid, 256)
        sums = jnp.dot(w2_ref[...], piece, preferred_element_type=f32)
        for k in range(R2):
            y = i * R2 + k
            t = y // 64 + 1
            at = lax.rem(2 * y, 128)
            a, b, c = (sums[(v * R2 + k) * outs : (v * R2 + k + 1) * outs] for v in range(3))
            west = roll(pedge[0, t], lax.rem(128 - at, 128))
            east = roll(pedge[1, t], 127 - at)
            a = jnp.where(lane8 == 0, jnp.concatenate([west, west], axis=1), roll(a, 1))
            c = jnp.where(lane8 == 255, jnp.concatenate([east, east], axis=1), roll(c, -1))
            m = jnp.broadcast_to(mask_ref[pl.ds(y, 1), :].astype(f32), (outs, 256))
            out_ref[y] = ((a + b + c + bias2) * m).astype(bf16)
        return 0

    lax.fori_loop(0, rows // R2, out_rows, 0, unroll=4)


def per_device(
    ocean_state, atm_blocks, dest_tile, dest_row, live_entry, land_mask, fold_pair, first_weight, first_bias,
    second_weight, second_bias,
):
    rows, levels4, cols = ocean_state.shape
    held, fields, block_cols = atm_blocks.shape
    g_y, g_x = lax.axis_size("gy"), lax.axis_size("gx")
    devices = g_y * g_x
    cap = max(2, 2 * held // devices)
    slots = devices * cap
    half = rows // 2
    cin = levels4 + fields
    hid, outs = first_weight.shape[2], second_weight.shape[2]
    tiles = rows // 64
    params = functools.partial(pltpu.CompilerParams, vmem_limit_bytes=60 * 2**20)

    assert half <= 256 and cap <= 128
    outgoing = pl.pallas_call(
        functools.partial(pack_kernel, empty=half),
        out_shape=jax.ShapeDtypeStruct((devices, cap + 1, fields, block_cols), bf16),
        in_specs=[smem(), smem(), smem(), vmem()],
        out_specs=vmem(),
        scratch_shapes=[pltpu.SMEM((devices,), jnp.int32), pltpu.VMEM((devices, 8, 128), f32)],
        name="pack",
    )(dest_tile.reshape(held), dest_row, live_entry, atm_blocks)
    incoming = lax.all_to_all(outgoing, ("gy", "gx"), split_axis=0, concat_axis=0, tiled=True)
    incoming_rows = incoming[:, cap, 0, :cap].astype(jnp.int32)
    spread = np.zeros((block_cols, cols), np.float32)
    spread[np.arange(cols) // 2, np.arange(cols)] = 1
    inputs, edge_cols = pl.pallas_call(
        combine_kernel,
        out_shape=(
            jax.ShapeDtypeStruct((rows, cin, cols), bf16),
            jax.ShapeDtypeStruct((2, tiles, cin, 128), bf16),
        ),
        in_specs=[smem()] + [vmem()] * 4,
        out_specs=(vmem(), vmem()),
        scratch_shapes=[pltpu.VMEM((half + 1, fields, block_cols), f32), pltpu.VMEM((half, fields, cols), f32)],
        compiler_params=params(),
        name="combine",
    )(
        incoming_rows.reshape(slots), incoming, ocean_state, land_mask,
        jnp.asarray(spread, bf16),
    )

    from_cols, rows_s, rows_n, top_all = pl.pallas_call(
        functools.partial(exchange_kernel, g_y, g_x),
        out_shape=(
            jax.ShapeDtypeStruct((2, tiles, cin, 128), bf16),
            jax.ShapeDtypeStruct((3, 2, cin, cols), bf16),
            jax.ShapeDtypeStruct((3, 2, cin, cols), bf16),
            jax.ShapeDtypeStruct((g_x, 2, cin, cols), bf16),
        ),
        in_specs=[anym(), anym()],
        out_specs=(anym(),) * 4,
        scratch_shapes=[
            pltpu.SemaphoreType.DMA((8 + g_x,)), pltpu.SemaphoreType.DMA((8 + g_x,)), pltpu.SemaphoreType.DMA,
        ],
        compiler_params=pltpu.CompilerParams(collective_id=0, has_side_effects=True),
        name="exchange",
    )(edge_cols, inputs)

    def band(r):
        t = np.zeros((3, r, r + 2), np.float32)
        for u in range(3):
            t[u, np.arange(r), np.arange(r) + u] = 1
        return jnp.asarray(t, bf16)

    w1 = jnp.einsum("urs,uvoc->vrosc", band(R1), first_weight).reshape(3, R1 * hid, (R1 + 2) * cin)
    w1s = first_weight.transpose(2, 0, 1, 3).reshape(hid, 9 * cin)
    w2 = jnp.einsum("urs,uvoc->vrosc", band(R2), second_weight).reshape(3 * R2 * outs, (R2 + 2) * hid)
    w2e = jnp.stack([second_weight[:, v].transpose(1, 0, 2).reshape(outs, 3 * hid) for v in (0, 2)])
    levels = levels4 // 4
    channel = np.arange(cin)
    negative = (channel < 2 * levels) | (channel == levels4) | (channel == levels4 + 1)
    signs = jnp.asarray(np.where(negative, -1.0, 1.0).astype(np.float32)[:, None])
    h_rows = -(-(rows + 2) // (GROUP * R1)) * (GROUP * R1)
    x_shape = (h_rows + 2, cin, cols)
    return pl.pallas_call(
        functools.partial(conv_kernel, g_y, g_x),
        out_shape=jax.ShapeDtypeStruct((rows, outs, cols), bf16),
        in_specs=[smem(), anym()] + [vmem()] * 13,
        out_specs=vmem(),
        scratch_shapes=[
            pltpu.VMEM(x_shape, bf16),
            pltpu.VMEM((2, tiles + 2, cin, 128), f32),
            pltpu.VMEM((h_rows, hid, cols), bf16),
            pltpu.VMEM((3, 2, cin, cols), f32),
            pltpu.VMEM((3, 2, cin, cols), f32),
            pltpu.VMEM((2, hid, 128 * (tiles + 2)), f32),
            pltpu.VMEM((2, tiles + 2, outs, 128), f32),
            pltpu.SemaphoreType.DMA,
        ],
        compiler_params=params(),
        name="conv",
    )(
        fold_pair, inputs, edge_cols, from_cols, rows_s, rows_n, top_all, land_mask, w1, w1s, first_bias[:, None], w2,
        w2e, second_bias[:, None], signs,
    )


def solution(mesh):
    return jax.shard_map(
        per_device,
        mesh=mesh,
        in_specs=(
            P("gy", None, "gx"),
            P(("gy", "gx"), None, None),
            P(("gy", "gx"), None),
            P(("gy", "gx")),
            P(("gy", "gx")),
            P("gy", "gx"),
            P(),
            P(),
            P(),
            P(),
            P(),
        ),
        out_specs=P("gy", None, "gx"),
        check_vma=False,
    )
```

```python
import functools

import jax
import jax.numpy as jnp
import numpy as np
from jax import lax
from jax.experimental import pallas as pl
from jax.experimental.pallas import tpu as pltpu
from jax.sharding import PartitionSpec as P

MESH = pl.DeviceIdType.MESH
R1 = 6
R2 = 6
GROUP = 5
f32 = jnp.float32
bf16 = jnp.bfloat16


def vmem():
    return pl.BlockSpec(memory_space=pltpu.VMEM)


def smem():
    return pl.BlockSpec(memory_space=pltpu.SMEM)


def anym():
    return pl.BlockSpec(memory_space=pl.ANY)


def pack_kernel(tile_ref, row_ref, live_ref, atm_ref, out_ref, count, names, *, empty):
    devices, cap = out_ref.shape[0], out_ref.shape[1] - 1
    names[...] = jnp.full(names.shape, empty, f32)
    lane = lax.broadcasted_iota(jnp.int32, (8, 128), 1)

    def clear(i, _):
        count[i] = 0
        return 0

    lax.fori_loop(0, devices, clear, 0, unroll=8)

    def place(e, _):
        t, live = tile_ref[e], live_ref[e]
        c = count[t]
        count[t] = c + live
        out_ref[t, jnp.where(live == 1, c, cap)] = atm_ref[e]
        names[t] = jnp.where(lane == jnp.where(live == 1, c, -1), row_ref[e].astype(f32), names[t])
        return 0

    lax.fori_loop(0, atm_ref.shape[0], place, 0, unroll=8)

    def name(t, _):
        out_ref[t, cap] = jnp.concatenate([names[t], names[t]], axis=0).astype(bf16)
        return 0

    lax.fori_loop(0, devices, name, 0, unroll=4)


def mask_rows(mask_ref, out_ref, values, done):
    rows, count, cols = out_ref.shape
    lane = lax.broadcasted_iota(jnp.int32, (count, 128), 1)

    def rows8(i, carry):
        lo, hi = carry
        m = mask_ref[pl.ds(i * 8, 8), :].astype(f32)
        for k in range(8):
            y = i * 8 + k
            full = values(i, k) * jnp.broadcast_to(m[k : k + 1, :], (count, cols))
            out_ref[y] = full.astype(bf16)
            at = lax.rem(2 * y, 128)
            here = (lane >> 1) == lax.rem(y, 64)
            lo = jnp.where(here, pltpu.roll(full[:, :128], at, 1), lo)
            hi = jnp.where(here, pltpu.roll(full[:, 128:], lax.rem(at + 2, 128), 1), hi)
        return lo, hi

    zero = jnp.zeros((count, 128), f32)

    def tile(t, _):
        lo, hi = lax.fori_loop(t * 8, t * 8 + 8, rows8, (zero, zero))
        done(t, lo.astype(bf16), hi.astype(bf16))
        return 0

    lax.fori_loop(0, rows // 64, tile, 0)


def state_kernel(state_ref, mask_ref, out_ref, cols_ref, ends_ref):
    rows = out_ref.shape[0]

    def done(t, lo, hi):
        cols_ref[0, t] = lo
        cols_ref[1, t] = hi

    mask_rows(mask_ref, out_ref, lambda i, k: state_ref[i * 8 + k].astype(f32), done)
    for j in range(2):
        ends_ref[0, j] = out_ref[j]
        ends_ref[1, j] = out_ref[rows - 2 + j]


def forcing_kernel(rows_ref, blocks_ref, mask_ref, up_ref, cs_ref, es_ref, out_ref, cols_ref, ends_ref, acc, up):
    half = acc.shape[0] - 1
    slots = blocks_ref.shape[1] - 1
    rows = out_ref.shape[0]
    acc[...] = jnp.zeros_like(acc)

    def add(d, _):
        for k in range(slots):
            r = rows_ref[d * slots + k]
            acc[r] += blocks_ref[d, k].astype(f32)
        return 0

    lax.fori_loop(0, blocks_ref.shape[0], add, 0)

    def spread(i, _):
        piece = acc[pl.ds(i * 16, 16)].astype(bf16).reshape(16 * 16, 128)
        wide = jnp.dot(piece, up_ref[...], preferred_element_type=f32)
        up[pl.ds(i * 16, 16)] = wide.reshape(16, 16, 256)
        return 0

    lax.fori_loop(0, half // 16, spread, 0, unroll=4)

    def done(t, lo, hi):
        cols_ref[0, t] = jnp.concatenate([cs_ref[0, t], lo], axis=0)
        cols_ref[1, t] = jnp.concatenate([cs_ref[1, t], hi], axis=0)

    mask_rows(mask_ref, out_ref, lambda i, k: up[i * 4 + k // 2], done)
    for j in range(2):
        ends_ref[0, j] = jnp.concatenate([es_ref[0, j], out_ref[j]], axis=0)
        ends_ref[1, j] = jnp.concatenate([es_ref[1, j], out_ref[rows - 2 + j]], axis=0)


def exchange_kernel(g_y, g_x, cols_ref, ends_ref, from_cols, rows_s, rows_n, top_all, send, recv, own):
    gy, gx = lax.axis_index("gy"), lax.axis_index("gx")
    west, east = lax.rem(gx + g_x - 1, g_x), lax.rem(gx + 1, g_x)
    low, high = ends_ref.at[0], ends_ref.at[1]
    is_top = gy == g_y - 1
    barrier = pltpu.get_barrier_semaphore()

    def copy(src, dst, s, r, y, x):
        return pltpu.make_async_remote_copy(
            src_ref=src, dst_ref=dst, send_sem=send.at[s], recv_sem=recv.at[r], device_id=(y, x), device_id_type=MESH
        )

    def signal(y, x):
        pl.semaphore_signal(barrier, inc=1, device_id=(y, x), device_id_type=MESH)

    sides = (west, gx, east)

    @pl.when(gy > 0)
    def _():
        for x in sides:
            signal(gy - 1, x)

    @pl.when(gy < g_y - 1)
    def _():
        for x in sides:
            signal(gy + 1, x)
        for x in (west, east):
            signal(gy, x)

    @pl.when(is_top)
    def _():
        def one(d, _):
            signal(gy, lax.rem(gx + d, g_x))
            return 0

        lax.fori_loop(1, g_x, one, 0)

    top, bottom = is_top.astype(jnp.int32), (gy == 0).astype(jnp.int32)
    pl.semaphore_wait(barrier, top * (g_x - 1) + (1 - top) * 5 + (1 - bottom) * 3)

    to_west = copy(cols_ref.at[0], from_cols.at[1], 0, 1, gy, west)
    to_east = copy(cols_ref.at[1], from_cols.at[0], 1, 0, gy, east)
    to_south = [copy(low, rows_n.at[2 - k], 2 + k, 5 + 2 - k, gy - 1, sides[k]) for k in range(3)]
    to_north = [copy(high, rows_s.at[2 - k], 5 + k, 2 + 2 - k, gy + 1, sides[k]) for k in range(3)]
    mine = pltpu.make_async_copy(high, top_all.at[gx], own)

    def top_copy(d):
        return copy(high, top_all.at[gx], 8 + d, 8 + d, gy, lax.rem(gx + d, g_x))

    @pl.when(is_top)
    def _():
        def one(d, _):
            top_copy(d).start()
            return 0

        mine.start()
        lax.fori_loop(1, g_x, one, 0)

    @pl.when(gy > 0)
    def _():
        for c in to_south:
            c.start()

    @pl.when(gy < g_y - 1)
    def _():
        for c in to_north:
            c.start()

    to_west.start()
    to_east.start()
    to_west.wait()
    to_east.wait()

    @pl.when(gy > 0)
    def _():
        for c in to_south:
            c.wait_send()
        for k in range(3):
            copy(high, rows_s.at[k], 5, 2 + k, gy, west).wait_recv()

    @pl.when(gy < g_y - 1)
    def _():
        for c in to_north:
            c.wait_send()
        for k in range(3):
            copy(low, rows_n.at[k], 2, 5 + k, gy, west).wait_recv()

    @pl.when(is_top)
    def _():
        def one(d, _):
            c = top_copy(d)
            c.wait_send()
            src = lax.rem(gx + g_x - d, g_x)
            copy(high, top_all.at[src], 8 + d, 8 + d, gy, src).wait_recv()
            return 0

        lax.fori_loop(1, g_x, one, 0)
        mine.wait()


def roll(x, shift, axis=1):
    if isinstance(shift, int):
        shift = shift % x.shape[axis]
        if shift == 0:
            return x
    return pltpu.roll(x, shift, axis)


def conv_kernel(
    g_y, g_x, fold_ref, state_ref, forcing_ref, cols_ref, from_ref, rs_ref, rn_ref, top_ref, mask_ref, w1_ref, w1s_ref, b1_ref, w2_ref,
    w2e_ref, b2_ref, sign_ref, out_ref, x_ref, far_ref, h_ref, north, south, edge, pedge, sem,
):
    gy, gx = lax.axis_index("gy"), lax.axis_index("gx")
    rows = out_ref.shape[0]
    hid = w1s_ref.shape[0]
    is_top = gy == g_y - 1
    split = state_ref.shape[1]
    loads = [
        pltpu.make_async_copy(r, x_ref.at[pl.ds(2, rows), pl.ds(i * split, r.shape[1])], sem.at[i])
        for i, r in enumerate((state_ref, forcing_ref))
    ]
    for load in loads:
        load.start()
    lane256 = lax.broadcasted_iota(jnp.int32, (32, 256), 1)
    lane128 = lax.broadcasted_iota(jnp.int32, (32, 128), 1)
    back = (
        lax.broadcasted_iota(jnp.int32, (256, 256), 0) + lax.broadcasted_iota(jnp.int32, (256, 256), 1) == 255
    ).astype(bf16)

    def mirror(v):
        return jnp.dot(v, back, preferred_element_type=f32)

    def top_row(t):
        return mirror(top_ref[t, 1]) * sign_ref[...]

    def put(x, west, east):
        left = jnp.where(lane256 == 0, jnp.concatenate([west, west], axis=1), roll(x, 1))
        right = jnp.where(lane256 == 255, jnp.concatenate([east, east], axis=1), roll(x, -1))
        return left, right

    def side_rows(first, mid, last):
        return put(mid, roll(first[:, 128:], 1), roll(last[:, :128], -1))

    for j in range(2):
        for k in range(3):
            south[k, j] = jnp.where(gy > 0, rs_ref[k, j].astype(f32), 0.0)

    @pl.when(jnp.logical_not(is_top))
    def _():
        for j in range(2):
            for k in range(3):
                north[k, j] = rn_ref[k, j].astype(f32)

    @pl.when(is_top)
    def _():
        for k in range(3):
            t = fold_ref[lax.rem(gx + g_x - 1 + k, g_x)]
            north[k, 0] = top_row(t)
            north[k, 1] = jnp.zeros((32, 256), f32)

    def ext_hi(r0, r1, s0, s1):
        return jnp.where(lane128 >= 126, r1, roll(r0, -2)), jnp.where(lane128 < 2, roll(s0, 2), roll(s1, 4))

    def ext_lo(r0, r1, s0, s1):
        return jnp.where(lane128 >= 126, roll(r1, 126), roll(r0, 124)), jnp.where(lane128 < 2, s0, roll(s1, 2))

    def strip(body, ends):
        first, last = ends
        return jnp.concatenate([first] + [body[t].astype(f32) for t in range(rows // 64)] + [last], axis=1)

    hi, lo = slice(128, 256), slice(0, 128)
    far_w = strip(from_ref.at[0], ext_hi(south[0, 0][:, hi], south[0, 1][:, hi], north[0, 0][:, hi], north[0, 1][:, hi]))
    own_w = strip(cols_ref.at[0], ext_lo(south[1, 0][:, lo], south[1, 1][:, lo], north[1, 0][:, lo], north[1, 1][:, lo]))
    own_e = strip(cols_ref.at[1], ext_hi(south[1, 0][:, hi], south[1, 1][:, hi], north[1, 0][:, hi], north[1, 1][:, hi]))
    far_e = strip(from_ref.at[1], ext_lo(south[2, 0][:, lo], south[2, 1][:, lo], north[2, 0][:, lo], north[2, 1][:, lo]))

    def hidden_of(parts):
        stack = jnp.concatenate([p.astype(bf16) for p in parts], axis=0)
        total = jnp.dot(w1s_ref[...], stack, preferred_element_type=f32)
        return jnp.maximum(total + b1_ref[...], 0.0)

    for t in range(rows // 64 + 2):
        far_ref[0, t] = far_w[:, 128 * t : 128 * t + 128]
        far_ref[1, t] = far_e[:, 128 * t : 128 * t + 128]
    west_parts, east_parts = [], []
    for u in range(3):
        s = -2 * (u - 1)
        west_parts += [roll(far_w, s), roll(far_w, s - 1), roll(own_w, s)]
        east_parts += [roll(own_e, s - 1), roll(far_e, s), roll(far_e, s - 1)]
    edge_lane = lax.broadcasted_iota(jnp.int32, (hid, 128 * (rows // 64 + 2)), 1)
    live = (edge_lane >= 128) | (gy > 0)
    edge[0] = jnp.where(live, hidden_of(west_parts), 0.0)
    edge[1] = jnp.where(live, hidden_of(east_parts), 0.0)

    for load in loads:
        load.wait()
    for j in range(2):
        x_ref[j] = south[1, j].astype(bf16)
        x_ref[rows + 2 + j] = north[1, j].astype(bf16)
    for at in range(rows + 4, x_ref.shape[0]):
        x_ref[at] = jnp.zeros((32, 256), bf16)

    bias1 = jnp.concatenate([b1_ref[...]] * R1, axis=0)
    weights = jnp.concatenate([w1_ref[v] for v in range(3)], axis=1)

    def hidden_rows(i, _):
        first = i * (GROUP * R1)
        shifted = []
        for k in range(GROUP * R1 + 2):
            at = 124 + 2 * (first + k)
            t, lane = at // 128, lax.rem(at, 128)
            x = x_ref[first + k]
            left, right = put(x.astype(f32), roll(far_ref[0, t], 127 - lane), roll(far_ref[1, t], 127 - lane))
            shifted.append((left.astype(bf16), x, right.astype(bf16)))
        for b in range(GROUP):
            piece = jnp.concatenate([row[v] for v in range(3) for row in shifted[b * R1 : b * R1 + R1 + 2]], axis=0)
            total = jnp.dot(weights, piece, preferred_element_type=f32)
            total = jnp.maximum(total + bias1, 0.0)
            h_ref[pl.ds(first + b * R1, R1)] = total.astype(bf16).reshape(R1, hid, 256)
        return 0

    lax.fori_loop(0, h_ref.shape[0] // (GROUP * R1), hidden_rows, 0)

    @pl.when(gy == 0)
    def _():
        h_ref[0] = jnp.zeros((hid, 256), bf16)

    @pl.when(is_top)
    def _():
        for k in range(3):
            q = fold_ref[lax.rem(gx + g_x - 1 + k, g_x)]
            qw, qe = lax.rem(q + g_x - 1, g_x), lax.rem(q + 1, g_x)
            parts = []
            for j in range(2):
                a, b, c = (top_ref[t, j].astype(f32) for t in (qw, q, qe))
                left, right = side_rows(a, b, c)
                parts += [left, b, right]
            a, b, c = (top_row(fold_ref[t]) for t in (qw, q, qe))
            left, right = side_rows(a, b, c)
            parts += [left, b, right]
            folded = mirror(hidden_of(parts).astype(bf16))
            if k == 1:
                h_ref[rows + 1] = folded.astype(bf16)
            else:
                tiles = rows // 64 + 1
                e = 0 if k == 0 else 1
                piece = roll(folded[:, 128:], 1) if k == 0 else folded[:, :128]
                edge[e, :, 128 * tiles :] = piece

    for e in range(2):
        h = edge[e]
        stack = jnp.concatenate([roll(h, -2 * (u - 1)).astype(bf16) for u in range(3)], axis=0)
        sums = jnp.dot(w2e_ref[e], stack, preferred_element_type=f32)
        for t in range(rows // 64 + 2):
            pedge[e, t] = sums[:, 128 * t : 128 * t + 128]

    outs = out_ref.shape[1]
    lane8 = lax.broadcasted_iota(jnp.int32, (outs, 256), 1)
    bias2 = b2_ref[...]

    def out_rows(i, _):
        piece = h_ref[pl.ds(i * R2, R2 + 2)].reshape((R2 + 2) * hid, 256)
        sums = jnp.dot(w2_ref[...], piece, preferred_element_type=f32)
        for k in range(R2):
            y = i * R2 + k
            t = y // 64 + 1
            at = lax.rem(2 * y, 128)
            a, b, c = (sums[(v * R2 + k) * outs : (v * R2 + k + 1) * outs] for v in range(3))
            west = roll(pedge[0, t], lax.rem(128 - at, 128))
            east = roll(pedge[1, t], 127 - at)
            a = jnp.where(lane8 == 0, jnp.concatenate([west, west], axis=1), roll(a, 1))
            c = jnp.where(lane8 == 255, jnp.concatenate([east, east], axis=1), roll(c, -1))
            m = jnp.broadcast_to(mask_ref[pl.ds(y, 1), :].astype(f32), (outs, 256))
            out_ref[y] = ((a + b + c + bias2) * m).astype(bf16)
        return 0

    lax.fori_loop(0, rows // R2, out_rows, 0, unroll=4)


def per_device(
    ocean_state, atm_blocks, dest_tile, dest_row, live_entry, land_mask, fold_pair, first_weight, first_bias,
    second_weight, second_bias,
):
    rows, levels4, cols = ocean_state.shape
    held, fields, block_cols = atm_blocks.shape
    g_y, g_x = lax.axis_size("gy"), lax.axis_size("gx")
    devices = g_y * g_x
    cap = max(2, 2 * held // devices)
    slots = devices * cap
    half = rows // 2
    cin = levels4 + fields
    hid, outs = first_weight.shape[2], second_weight.shape[2]
    tiles = rows // 64
    params = functools.partial(pltpu.CompilerParams, vmem_limit_bytes=60 * 2**20)

    assert half <= 256 and cap <= 128
    outgoing = pl.pallas_call(
        functools.partial(pack_kernel, empty=half),
        out_shape=jax.ShapeDtypeStruct((devices, cap + 1, fields, block_cols), bf16),
        in_specs=[smem(), smem(), smem(), vmem()],
        out_specs=vmem(),
        scratch_shapes=[pltpu.SMEM((devices,), jnp.int32), pltpu.VMEM((devices, 8, 128), f32)],
        name="pack",
    )(dest_tile.reshape(held), dest_row, live_entry, atm_blocks)
    incoming = lax.all_to_all(outgoing, ("gy", "gx"), split_axis=0, concat_axis=0, tiled=True)
    incoming_rows = incoming[:, cap, 0, :cap].astype(jnp.int32)
    spread = np.zeros((block_cols, cols), np.float32)
    spread[np.arange(cols) // 2, np.arange(cols)] = 1
    state, state_cols, state_ends = pl.pallas_call(
        state_kernel,
        out_shape=(
            jax.ShapeDtypeStruct((rows, levels4, cols), bf16),
            jax.ShapeDtypeStruct((2, tiles, levels4, 128), bf16),
            jax.ShapeDtypeStruct((2, 2, levels4, cols), bf16),
        ),
        in_specs=[vmem()] * 2,
        out_specs=(vmem(),) * 3,
        compiler_params=params(),
        cost_estimate=pl.CostEstimate(flops=rows * levels4 * cols * 8, bytes_accessed=rows * levels4 * cols * 4, transcendentals=0),
        name="state",
    )(ocean_state, land_mask)
    forcing, edge_cols, ends = pl.pallas_call(
        forcing_kernel,
        out_shape=(
            jax.ShapeDtypeStruct((rows, fields, cols), bf16),
            jax.ShapeDtypeStruct((2, tiles, cin, 128), bf16),
            jax.ShapeDtypeStruct((2, 2, cin, cols), bf16),
        ),
        in_specs=[smem()] + [vmem()] * 5,
        out_specs=(vmem(),) * 3,
        scratch_shapes=[pltpu.VMEM((half + 1, fields, block_cols), f32), pltpu.VMEM((half, fields, cols), f32)],
        compiler_params=params(),
        name="forcing",
    )(incoming_rows.reshape(slots), incoming, land_mask, jnp.asarray(spread, bf16), state_cols, state_ends)

    from_cols, rows_s, rows_n, top_all = pl.pallas_call(
        functools.partial(exchange_kernel, g_y, g_x),
        out_shape=(
            jax.ShapeDtypeStruct((2, tiles, cin, 128), bf16),
            jax.ShapeDtypeStruct((3, 2, cin, cols), bf16),
            jax.ShapeDtypeStruct((3, 2, cin, cols), bf16),
            jax.ShapeDtypeStruct((g_x, 2, cin, cols), bf16),
        ),
        in_specs=[anym(), anym()],
        out_specs=(anym(),) * 4,
        scratch_shapes=[
            pltpu.SemaphoreType.DMA((8 + g_x,)), pltpu.SemaphoreType.DMA((8 + g_x,)), pltpu.SemaphoreType.DMA,
        ],
        compiler_params=pltpu.CompilerParams(collective_id=0, has_side_effects=True),
        name="exchange",
    )(edge_cols, ends)

    def band(r):
        t = np.zeros((3, r, r + 2), np.float32)
        for u in range(3):
            t[u, np.arange(r), np.arange(r) + u] = 1
        return jnp.asarray(t, bf16)

    w1 = jnp.einsum("urs,uvoc->vrosc", band(R1), first_weight).reshape(3, R1 * hid, (R1 + 2) * cin)
    w1s = first_weight.transpose(2, 0, 1, 3).reshape(hid, 9 * cin)
    w2 = jnp.einsum("urs,uvoc->vrosc", band(R2), second_weight).reshape(3 * R2 * outs, (R2 + 2) * hid)
    w2e = jnp.stack([second_weight[:, v].transpose(1, 0, 2).reshape(outs, 3 * hid) for v in (0, 2)])
    levels = levels4 // 4
    channel = np.arange(cin)
    negative = (channel < 2 * levels) | (channel == levels4) | (channel == levels4 + 1)
    signs = jnp.asarray(np.where(negative, -1.0, 1.0).astype(np.float32)[:, None])
    h_rows = -(-(rows + 2) // (GROUP * R1)) * (GROUP * R1)
    x_shape = (h_rows + 2, cin, cols)
    return pl.pallas_call(
        functools.partial(conv_kernel, g_y, g_x),
        out_shape=jax.ShapeDtypeStruct((rows, outs, cols), bf16),
        in_specs=[smem(), anym(), anym()] + [vmem()] * 13,
        out_specs=vmem(),
        scratch_shapes=[
            pltpu.VMEM(x_shape, bf16),
            pltpu.VMEM((2, tiles + 2, cin, 128), f32),
            pltpu.VMEM((h_rows, hid, cols), bf16),
            pltpu.VMEM((3, 2, cin, cols), f32),
            pltpu.VMEM((3, 2, cin, cols), f32),
            pltpu.VMEM((2, hid, 128 * (tiles + 2)), f32),
            pltpu.VMEM((2, tiles + 2, outs, 128), f32),
            pltpu.SemaphoreType.DMA((2,)),
        ],
        compiler_params=params(),
        name="conv",
    )(
        fold_pair, state, forcing, edge_cols, from_cols, rows_s, rows_n, top_all, land_mask, w1, w1s, first_bias[:, None], w2,
        w2e, second_bias[:, None], signs,
    )


def solution(mesh):
    return jax.shard_map(
        per_device,
        mesh=mesh,
        in_specs=(
            P("gy", None, "gx"),
            P(("gy", "gx"), None, None),
            P(("gy", "gx"), None),
            P(("gy", "gx")),
            P(("gy", "gx")),
            P("gy", "gx"),
            P(),
            P(),
            P(),
            P(),
            P(),
        ),
        out_specs=P("gy", None, "gx"),
        check_vma=False,
    )
```
